32 devices in a mesh: grp: 2 (over y), sub: 4 (over z), ex: 4 (over x, core).
Axes of the slice: x: 2, y: 2, z: 4, core: 2. Of those that a mesh axis runs over, the one named last changes fastest.
Arguments:
- design: bfloat16 [2560, 28672], P('sub', 'ex'), as said below
- margins: float32 [2560, 512], P('sub'), may hold values from -6 to 6
- test_ids: int32 [512], P('grp'), parts along dimension 0, may hold values from 0 to 511
- l1_penalty: float32 [512], P('grp'), parts along dimension 0, may hold values from 0.05 to 1
- l2_penalty: float32 [512], P('grp'), parts along dimension 0, may hold values from 0.1 to 3
Outputs:
- coefficients: float32 [4, 7168, 512], P('ex', 'sub', 'grp'), parts along dimension 2
The draws below stay inside these ranges and needn't reach their ends.
There are 2 independent parts, one for each index of `grp`. The reference program is written for one: setup_inputs(seed, part) draws one part's arguments, and reference() takes and returns one part's arrays. A program takes and returns all parts, laid end to end along the dimension named above; an argument that names none is the same for every part. Nothing has to cross between parts.
Inputs may be any that keep to these rules, and one draw needn't show every extreme that they name: `design`: each entry is (m - a) / sqrt(a (1 - a)) / sqrt(2560) for a 0/1 inclusion m and a fixed inclusion rate a of the draw.
All inputs are finite; a program needn't handle non-finite values.
Results may differ from the reference program's by a relative error of at most 0.007.
Values may be sent and summed in bfloat16 or wider, within the bound.
A program may use at most 64 MiB of HBM per device.

```python
import math
import jax
import jax.numpy as jnp
from jax import lax

N = 28672
P_SIZE = 256
PT = 512
SUB_DEV = 640
SUBSETS = 2560
N_EX = 4


def draw_design(key, part):
    key = jax.random.fold_in(key, 11)
    rate = 0.5
    inclusion = jax.random.bernoulli(key, rate, (SUBSETS, N)).astype(jnp.float32)
    scaled = (inclusion - rate) / math.sqrt(rate * (1.0 - rate) * SUBSETS)
    return scaled.astype(jnp.bfloat16)


def set_ends(values, rng, least, top_value):
    dims = values.shape
    index_at = [jax.random.randint(jax.random.fold_in(rng, axis), (), 0, dims[axis]) for axis in range(len(dims))]
    values = values.at[tuple(index_at)].set(least)
    longest = dims.index(max(dims))
    index_at[longest] = (index_at[longest] + 1) % dims[longest]
    return values.at[tuple(index_at)].set(top_value)


def block_scale(stream_key, shape, cuts, least, largest):
    loudness = 1.0
    for dim, shards_of in cuts:
        steps = jax.random.uniform(jax.random.fold_in(jax.random.fold_in(stream_key, 6), dim), (shards_of,), jnp.float32, least / len(cuts), largest / len(cuts))
        loudness = loudness * jnp.repeat(jnp.exp(steps), shape[dim] // shards_of).reshape((-1,) + (1,) * (len(shape) - 1 - dim))
    return loudness


def gaussian(stream_key, shape, deviation, bound, split=(), dtype=jnp.bfloat16):
    values = jax.random.normal(stream_key, shape, jnp.float32) * deviation
    if len(split) > 0:
        values = block_scale(stream_key, shape, split, -0.22, 0.18) * values
    return jnp.clip(values, min=-bound, max=bound).astype(dtype)


def setup_inputs(seed: int = 0, part: int = 0) -> dict:
    arg_keys = jax.random.split(jax.random.key(seed), 6)
    own_keys = jax.random.split(jax.random.fold_in(arg_keys[5], part), 6)
    design = draw_design(jax.random.fold_in(arg_keys[5], 71), part)
    margins = gaussian(arg_keys[1], (SUBSETS, PT), 1.0, 6.0, ((0, 4),), jnp.float32)
    test_ids = set_ends(jax.random.randint(own_keys[2], (P_SIZE,), 0, PT), jax.random.fold_in(own_keys[2], 1), 0, PT - 1).astype(jnp.int32)
    l1_penalty = jnp.clip(jnp.exp(jax.random.uniform(own_keys[3], (P_SIZE,), jnp.float32, math.log(0.05), math.log(1.0))), 0.05, 1.0)
    l2_penalty = jnp.clip(jnp.exp(jax.random.uniform(own_keys[4], (P_SIZE,), jnp.float32, math.log(0.1), math.log(3.0))), 0.1, 3.0)
    return {"design": design, "margins": margins, "test_ids": test_ids, "l1_penalty": l1_penalty, "l2_penalty": l2_penalty}


step_size = 0.3


def shrink(values, l1_penalty, l2_penalty):
    limit = step_size * l1_penalty
    kept = jnp.maximum(values - limit, 0.0) - jnp.maximum(-values - limit, 0.0)
    return kept / (1.0 + step_size * l2_penalty)


def reference(design, margins, test_ids, l1_penalty, l2_penalty):
    target = jnp.take(margins, test_ids.astype(jnp.int32), axis=1)
    blocks = design.reshape(SUBSETS // SUB_DEV, SUB_DEV, N)

    def gradient(resid_half):
        stacked = resid_half.reshape(SUBSETS // SUB_DEV, SUB_DEV, P_SIZE)

        def add_block(summed, operands):
            product = lax.dot_general(operands[0], operands[1], (((0,), (0,)), ((), ())), preferred_element_type=jnp.float32)
            return summed + product, None

        summed, unused = lax.scan(add_block, jnp.zeros((N, P_SIZE), jnp.float32), (blocks, stacked))
        return summed

    def predict(coef_half):
        return lax.map(lambda row_block: jnp.dot(row_block, coef_half, preferred_element_type=jnp.float32), blocks).reshape(SUBSETS, P_SIZE)

    start = (-target).astype(jnp.bfloat16)
    coef_one = shrink(-step_size * gradient(start), l1_penalty, l2_penalty)
    resid = predict(coef_one.astype(jnp.bfloat16)) - target
    coef_two = shrink(coef_one - step_size * gradient(resid.astype(jnp.bfloat16)), l1_penalty, l2_penalty)
    return coef_two.reshape(N_EX, N // N_EX, P_SIZE)
```

```python
import functools

import jax
import jax.numpy as jnp
from jax import lax
from jax.experimental import pallas as pl
from jax.experimental.pallas import tpu as pltpu
from jax.sharding import PartitionSpec as P

step_size = 0.3
MESH = pl.DeviceIdType.MESH
CHUNK = 256
AHEAD = 3
F32 = jnp.float32
BF16 = jnp.bfloat16


def shrink(values, l1_penalty, l2_penalty):
    limit = step_size * l1_penalty
    kept = jnp.maximum(values - limit, 0.0) - jnp.maximum(-values - limit, 0.0)
    return kept / (1.0 + step_size * l2_penalty)


def gathered(design, margins, test_ids, l1_penalty, l2_penalty):
    target = jnp.take(margins, test_ids, axis=1)
    start = (-target).astype(BF16)

    def gradient_rows(resid_half):
        return lax.psum_scatter(
            lax.dot_general(design, resid_half, (((0,), (0,)), ((), ())), preferred_element_type=F32),
            "sub",
            scatter_dimension=0,
            tiled=True,
        )

    coef_one = shrink(-step_size * gradient_rows(start), l1_penalty, l2_penalty)
    predicted = jnp.dot(
        design,
        lax.all_gather(coef_one.astype(BF16), "sub", axis=0, tiled=True),
        preferred_element_type=F32,
    )
    summed = lax.psum(predicted, "ex")
    resid_half = (summed - target).astype(BF16)
    coef_two = shrink(coef_one - step_size * gradient_rows(resid_half), l1_penalty, l2_penalty)
    return coef_two[None]


def kernel(
    n_sub, chunks, design, margins, ids, l1, l2, out,
    full, start, target, pred, coef,
    send_a, recv_a, keep_b, send_b, recv_b, keep_c, send_c, recv_c, resid,
    own_sem, z_send, z_recv, y_send, y_recv, s_send, s_recv, e_send, e_recv, r_send, r_recv, c_send, c_recv, d_send, d_recv,
):
    g = lax.axis_index("grp")
    s = lax.axis_index("sub")
    e = lax.axis_index("ex")
    core = lax.rem(e, 2)
    col = lax.div(e, 2)
    rows = design.shape[0]
    half = rows // 2
    tests = out.shape[0]
    width = chunks * CHUNK
    part = tests // 4
    own = part // n_sub

    def to_sub(k):
        return {"sub": lax.rem(s + k, n_sub)}

    def to_ex(j):
        return {"ex": lax.rem(e + j, 4)}

    to_core = {"ex": col * 2 + 1 - core}
    to_col = {"ex": (1 - col) * 2 + core}
    to_grp = {"grp": 1 - g}

    def remote(src, dst, send, recv, device):
        return pltpu.make_async_remote_copy(
            src_ref=src, dst_ref=dst, send_sem=send, recv_sem=recv, device_id=device, device_id_type=MESH
        )

    barrier = pltpu.get_barrier_semaphore()
    for device in [to_sub(k) for k in range(1, n_sub)] + [to_ex(j) for j in range(1, 4)] + [to_grp]:
        pl.semaphore_signal(barrier, inc=1, device_id=device, device_id_type=MESH)
    pl.semaphore_wait(barrier, n_sub + 3)

    def own_copy(c):
        return pltpu.make_async_copy(
            design.at[:, pl.ds(pl.multiple_of(s * width + c * CHUNK, CHUNK), CHUNK)],
            full.at[c, s],
            own_sem.at[c],
        )

    def z_copy(c, k):
        peer = lax.rem(s + k, n_sub)
        return remote(
            design.at[pl.ds(pl.multiple_of(g * half, 16), half), pl.ds(pl.multiple_of(peer * width + c * CHUNK, CHUNK), CHUNK)],
            full.at[c, s, pl.ds(pl.multiple_of(g * half, 16), half)],
            z_send.at[c, k - 1],
            z_recv.at[c, k - 1],
            {"sub": peer},
        )

    def y_copy(c, k):
        block = full.at[c, lax.rem(s + n_sub - k, n_sub), pl.ds(pl.multiple_of(g * half, 16), half)]
        return remote(block, block, y_send.at[c, k - 1], y_recv.at[c, k - 1], to_grp)

    hops = range(1, n_sub)
    hot = (lax.broadcasted_iota(jnp.int32, (tests, margins.shape[1]), 1) == ids[...]).astype(F32)
    own_target = lax.dot_general(
        hot, margins[...], (((1,), (1,)), ((), ())), precision=lax.Precision.HIGHEST, preferred_element_type=F32
    )
    target[...] = own_target
    start[s] = (-own_target).astype(BF16)

    quarter = pl.ds(pl.multiple_of(e * part, 16), part)

    def s_copy(k):
        block = start.at[s, quarter]
        return remote(block, block, s_send.at[k - 1], s_recv.at[k - 1], to_sub(k))

    def e_copy(j, k):
        block = start.at[lax.rem(s + k, n_sub), quarter]
        return remote(block, block, e_send.at[j - 1, k - 1], e_recv.at[j - 1, k - 1], to_ex(j))

    for k in hops:
        s_copy(k).start()
    for c in range(min(AHEAD, chunks)):
        for k in hops:
            z_copy(c, k).start()
    for c in range(chunks):
        own_copy(c).start()
    for k in hops:
        s_copy(k).wait()
    for j in range(1, 4):
        for k in hops:
            e_copy(j, k).start()

    first = jnp.where(e == 0, 1.0, 0.0).astype(F32)
    for i in range(n_sub):
        pred[i] = jnp.zeros(pred.shape[1:], F32)
    pred[s] = target[...] * (-first)
    limit = step_size * l1[...]
    scale = 1.0 / (1.0 + step_size * l2[...])

    def prox(values):
        return (jnp.maximum(values - limit, 0.0) - jnp.maximum(-values - limit, 0.0)) * scale

    for j in range(1, 4):
        for k in hops:
            e_copy(j, k).wait()

    def pass_on(c):
        for k in hops:
            z_copy(c, k).wait()
            y_copy(c, k).start()

    def work(c):
        own_copy(c).wait()
        for k in hops:
            y_copy(c, k).wait()
        grad = jnp.dot(start[0], full[c, 0], preferred_element_type=F32)
        for i in range(1, n_sub):
            grad += jnp.dot(start[i], full[c, i], preferred_element_type=F32)
        one = prox(-step_size * grad)
        coef[c] = one
        one_half = one.astype(BF16)
        for i in range(n_sub):
            pred[i] += lax.dot_general(one_half, full[c, i], (((1,), (1,)), ((), ())), preferred_element_type=F32)

    pass_on(0)

    def step(c, carry):
        @pl.when(c + AHEAD - 1 < chunks)
        def _():
            for k in hops:
                z_copy(c + AHEAD - 1, k).start()

        pass_on(c)
        work(c - 1)
        return carry

    lax.fori_loop(1, chunks, step, 0)
    work(chunks - 1)

    def rows_of(first_row, count):
        return pl.ds(pl.multiple_of(first_row, 16), count)

    def a_copy(i):
        return remote(send_a.at[i], recv_a.at[i], r_send.at[0, i], r_recv.at[0, i], to_core)

    def b_copy(i):
        return remote(send_b.at[i], recv_b.at[i], r_send.at[1, i], r_recv.at[1, i], to_col)

    def c_copy(i, k):
        peer = lax.rem(s + k, n_sub)
        return remote(
            send_c.at[i, rows_of(peer * own, own)], recv_c.at[i, k - 1], c_send.at[i, k - 1], c_recv.at[i, k - 1], to_sub(k)
        )

    base = core * (2 * part) + col * part

    def d_copy(i, k):
        block = resid.at[i, rows_of(base + s * own, own)]
        return remote(block, block, d_send.at[i, k - 1], d_recv.at[i, k - 1], to_sub(k))

    def e2_copy(i):
        block = resid.at[i, rows_of(base, part)]
        return remote(block, block, r_send.at[2, i], r_recv.at[2, i], to_col)

    def f_copy(i):
        block = resid.at[i, rows_of(core * (2 * part), 2 * part)]
        return remote(block, block, r_send.at[3, i], r_recv.at[3, i], to_core)

    def stage_a(i):
        send_a[i] = pred[i, rows_of((1 - core) * (2 * part), 2 * part)].astype(BF16)
        a_copy(i).start()

    def stage_b(i):
        a_copy(i).wait()
        there = rows_of((1 - col) * part, part)
        here = rows_of(col * part, part)
        send_b[i] = (pred[i, rows_of(core * (2 * part) + (1 - col) * part, part)] + recv_a[i, there].astype(F32)).astype(BF16)
        b_copy(i).start()
        keep_b[i] = pred[i, rows_of(base, part)] + recv_a[i, here].astype(F32)

    def stage_c(i):
        b_copy(i).wait()
        total = keep_b[i] + recv_b[i].astype(F32)
        send_c[i] = total.astype(BF16)
        for k in hops:
            c_copy(i, k).start()
        keep_c[i] = total

    def stage_d(i):
        total = keep_c[i, rows_of(s * own, own)]
        for k in hops:
            c_copy(i, k).wait()
            total += recv_c[i, k - 1].astype(F32)
        resid[i, rows_of(base + s * own, own)] = total.astype(BF16)
        for k in hops:
            d_copy(i, k).start()

    def stage_e(i):
        for k in hops:
            d_copy(i, k).wait()
        e2_copy(i).start()

    def stage_f(i):
        e2_copy(i).wait()
        f_copy(i).start()

    stages = [stage_a, stage_b, stage_c, stage_d, stage_e, stage_f]
    for t in range(n_sub + len(stages) - 1):
        for number in reversed(range(len(stages))):
            if 0 <= t - number < n_sub:
                stages[number](t - number)
    for i in range(n_sub):
        f_copy(i).wait()

    def finish(c, carry):
        grad = jnp.dot(resid[0], full[c, 0], preferred_element_type=F32)
        for i in range(1, n_sub):
            grad += jnp.dot(resid[i], full[c, i], preferred_element_type=F32)
        out[:, pl.ds(pl.multiple_of(c * CHUNK, CHUNK), CHUNK)] = prox(coef[c] - step_size * grad)
        return carry

    lax.fori_loop(0, chunks, finish, 0)


def transposed(n_sub, design, margins, test_ids, l1_penalty, l2_penalty):
    rows = design.shape[0]
    width = design.shape[1] // n_sub
    chunks = width // CHUNK
    tests = test_ids.shape[0]
    part = tests // 4
    own = part // n_sub
    vmem = pl.BlockSpec(memory_space=pltpu.VMEM)
    dma = pltpu.SemaphoreType.DMA
    coef_two = pl.pallas_call(
        functools.partial(kernel, n_sub, chunks),
        out_shape=jax.ShapeDtypeStruct((tests, width), F32),
        in_specs=[pl.BlockSpec(memory_space=pl.ANY)] + [vmem] * 4,
        out_specs=vmem,
        scratch_shapes=[
            pltpu.VMEM((chunks, n_sub, rows, CHUNK), BF16),
            pltpu.VMEM((n_sub, tests, rows), BF16),
            pltpu.VMEM((tests, rows), F32),
            pltpu.VMEM((n_sub, tests, rows), F32),
            pltpu.VMEM((chunks, tests, CHUNK), F32),
            pltpu.VMEM((n_sub, 2 * part, rows), BF16),
            pltpu.VMEM((n_sub, 2 * part, rows), BF16),
            pltpu.VMEM((n_sub, part, rows), F32),
            pltpu.VMEM((n_sub, part, rows), BF16),
            pltpu.VMEM((n_sub, part, rows), BF16),
            pltpu.VMEM((n_sub, part, rows), F32),
            pltpu.VMEM((n_sub, part, rows), BF16),
            pltpu.VMEM((n_sub, n_sub - 1, own, rows), BF16),
            pltpu.VMEM((n_sub, tests, rows), BF16),
            dma((chunks,)),
            dma((chunks, n_sub - 1)),
            dma((chunks, n_sub - 1)),
            dma((chunks, n_sub - 1)),
            dma((chunks, n_sub - 1)),
            dma((n_sub - 1,)),
            dma((n_sub - 1,)),
            dma((3, n_sub - 1)),
            dma((3, n_sub - 1)),
            dma((4, n_sub)),
            dma((4, n_sub)),
            dma((n_sub, n_sub - 1)),
            dma((n_sub, n_sub - 1)),
            dma((n_sub, n_sub - 1)),
            dma((n_sub, n_sub - 1)),
        ],
        compiler_params=pltpu.CompilerParams(
            collective_id=0, has_side_effects=True, vmem_limit_bytes=48 * 1024 * 1024
        ),
    )(design, margins, test_ids[:, None], l1_penalty[:, None], l2_penalty[:, None])
    return coef_two.T[None]


def solution(mesh):
    n_sub = mesh.shape["sub"]

    def local(design, margins, test_ids, l1_penalty, l2_penalty):
        width = design.shape[1] // n_sub
        fits = (
            mesh.shape["grp"] == 2
            and mesh.shape["ex"] == 4
            and n_sub > 1
            and width % CHUNK == 0
            and design.shape[0] % 128 == 0
            and test_ids.shape[0] % (64 * n_sub) == 0
        )
        if fits:
            return transposed(n_sub, design, margins, test_ids, l1_penalty, l2_penalty)
        return gathered(design, margins, test_ids, l1_penalty, l2_penalty)

    in_specs = (P("sub", "ex"), P("sub", None), P("grp"), P("grp"), P("grp"))
    out_specs = P("ex", "sub", "grp")
    return jax.shard_map(local, mesh=mesh, in_specs=in_specs, out_specs=out_specs, check_vma=False)
```

```python
import functools

import jax
import jax.numpy as jnp
from jax import lax
from jax.experimental import pallas as pl
from jax.experimental.pallas import tpu as pltpu
from jax.sharding import PartitionSpec as P

step_size = 0.3
MESH = pl.DeviceIdType.MESH
CHUNK = 256
AHEAD = 2
PIECES = 2
F32 = jnp.float32
BF16 = jnp.bfloat16


def shrink(values, l1_penalty, l2_penalty):
    limit = step_size * l1_penalty
    kept = jnp.maximum(values - limit, 0.0) - jnp.maximum(-values - limit, 0.0)
    return kept / (1.0 + step_size * l2_penalty)


def gathered(design, margins, test_ids, l1_penalty, l2_penalty):
    target = jnp.take(margins, test_ids, axis=1)
    start = (-target).astype(BF16)

    def gradient_rows(resid_half):
        return lax.psum_scatter(
            lax.dot_general(design, resid_half, (((0,), (0,)), ((), ())), preferred_element_type=F32),
            "sub",
            scatter_dimension=0,
            tiled=True,
        )

    coef_one = shrink(-step_size * gradient_rows(start), l1_penalty, l2_penalty)
    predicted = jnp.dot(
        design,
        lax.all_gather(coef_one.astype(BF16), "sub", axis=0, tiled=True),
        preferred_element_type=F32,
    )
    summed = lax.psum(predicted, "ex")
    resid_half = (summed - target).astype(BF16)
    coef_two = shrink(coef_one - step_size * gradient_rows(resid_half), l1_penalty, l2_penalty)
    return coef_two[None]


def kernel(
    n_sub, chunks, design, margins, ids, l1, l2, out,
    full, start, target, pred, coef, table, table_sem,
    send_a, recv_a, keep_b, send_b, recv_b, keep_c, send_c, recv_c, resid,
    own_sem, z_send, z_recv, y_send, y_recv, s_send, s_recv, e_send, e_recv, r_send, r_recv, c_send, c_recv, d_send, d_recv,
):
    g = lax.axis_index("grp")
    s = lax.axis_index("sub")
    e = lax.axis_index("ex")
    core = lax.rem(e, 2)
    col = lax.div(e, 2)
    rows = design.shape[0]
    half = rows // 2
    tests = out.shape[0]
    width = chunks * CHUNK
    part = tests // 4
    own = part // n_sub

    def to_sub(k):
        return {"sub": lax.rem(s + k, n_sub)}

    def to_ex(j):
        return {"ex": lax.rem(e + j, 4)}

    to_core = {"ex": col * 2 + 1 - core}
    to_col = {"ex": (1 - col) * 2 + core}
    to_grp = {"grp": 1 - g}

    def remote(src, dst, send, recv, device):
        return pltpu.make_async_remote_copy(
            src_ref=src, dst_ref=dst, send_sem=send, recv_sem=recv, device_id=device, device_id_type=MESH
        )

    barrier = pltpu.get_barrier_semaphore()
    for device in [to_sub(k) for k in range(1, n_sub)] + [to_ex(j) for j in range(1, 4)] + [to_grp]:
        pl.semaphore_signal(barrier, inc=1, device_id=device, device_id_type=MESH)

    fetch = pltpu.make_async_copy(margins, table, table_sem)
    fetch.start()
    eye = lax.broadcasted_iota(jnp.int32, (tests, tests), 0) == lax.broadcasted_iota(jnp.int32, (tests, tests), 1)

    def column(row):
        return jnp.sum(jnp.where(eye, row, 0.0), axis=1, keepdims=True)

    limit = step_size * column(l1[...])
    scale = 1.0 / (1.0 + step_size * column(l2[...]))
    wanted = column(ids[...].astype(F32))
    hot = (lax.broadcasted_iota(jnp.int32, (tests, margins.shape[1]), 1).astype(F32) == wanted).astype(F32)
    fetch.wait()
    own_target = lax.dot_general(
        hot, table[...], (((1,), (1,)), ((), ())), precision=lax.Precision.HIGHEST, preferred_element_type=F32
    )
    target[...] = own_target
    start[s] = (-own_target).astype(BF16)
    first = jnp.where(e == 0, 1.0, 0.0).astype(F32)
    for i in range(n_sub):
        pred[i] = jnp.zeros(pred.shape[1:], F32)
    pred[s] = target[...] * (-first)
    pl.semaphore_wait(barrier, n_sub + 3)

    def own_copy(c):
        return pltpu.make_async_copy(
            design.at[:, pl.ds(pl.multiple_of(s * width + c * CHUNK, CHUNK), CHUNK)],
            full.at[c, s],
            own_sem.at[c],
        )

    piece = half // PIECES

    def rows_at(h):
        return pl.ds(pl.multiple_of(g * half + h * piece, 16), piece)

    def z_copy(c, h, k):
        peer = lax.rem(s + k, n_sub)
        return remote(
            design.at[rows_at(h), pl.ds(pl.multiple_of(peer * width + c * CHUNK, CHUNK), CHUNK)],
            full.at[c, s, rows_at(h)],
            z_send.at[c, h, k - 1],
            z_recv.at[c, h, k - 1],
            {"sub": peer},
        )

    def y_copy(c, h, k):
        block = full.at[c, lax.rem(s + n_sub - k, n_sub), rows_at(h)]
        return remote(block, block, y_send.at[c, h, k - 1], y_recv.at[c, h, k - 1], to_grp)

    def send_chunk(c):
        for h in range(PIECES):
            for k in hops:
                z_copy(c, h, k).start()

    hops = range(1, n_sub)
    quarter = pl.ds(pl.multiple_of(e * part, 16), part)

    def s_copy(k):
        block = start.at[s, quarter]
        return remote(block, block, s_send.at[k - 1], s_recv.at[k - 1], to_sub(k))

    def e_copy(j, k):
        block = start.at[lax.rem(s + k, n_sub), quarter]
        return remote(block, block, e_send.at[j - 1, k - 1], e_recv.at[j - 1, k - 1], to_ex(j))

    for k in hops:
        s_copy(k).start()
    for c in range(min(AHEAD, chunks)):
        send_chunk(c)
    for c in range(chunks):
        own_copy(c).start()
    for k in hops:
        s_copy(k).wait()
    for j in range(1, 4):
        for k in hops:
            e_copy(j, k).start()

    def prox(values):
        return (jnp.maximum(values - limit, 0.0) - jnp.maximum(-values - limit, 0.0)) * scale

    def pass_on(c):
        for h in range(PIECES):
            for k in hops:
                z_copy(c, h, k).wait()
                y_copy(c, h, k).start()

    def work(c):
        own_copy(c).wait()
        for h in range(PIECES):
            for k in hops:
                y_copy(c, h, k).wait()
        grad = jnp.dot(start[0], full[c, 0], preferred_element_type=F32)
        for i in range(1, n_sub):
            grad += jnp.dot(start[i], full[c, i], preferred_element_type=F32)
        one = prox(-step_size * grad)
        coef[c] = one
        one_half = one.astype(BF16)
        for i in range(n_sub):
            pred[i] += lax.dot_general(one_half, full[c, i], (((1,), (1,)), ((), ())), preferred_element_type=F32)

    pass_on(0)
    for j in range(1, 4):
        for k in hops:
            e_copy(j, k).wait()

    def step(c, carry):
        @pl.when(c + AHEAD - 1 < chunks)
        def _():
            send_chunk(c + AHEAD - 1)

        pass_on(c)
        work(c - 1)
        return carry

    lax.fori_loop(1, chunks, step, 0)
    work(chunks - 1)

    def rows_of(first_row, count):
        return pl.ds(pl.multiple_of(first_row, 16), count)

    def a_copy(i):
        return remote(send_a.at[i], recv_a.at[i], r_send.at[0, i], r_recv.at[0, i], to_core)

    def b_copy(i):
        return remote(send_b.at[i], recv_b.at[i], r_send.at[1, i], r_recv.at[1, i], to_col)

    def c_copy(i, k):
        peer = lax.rem(s + k, n_sub)
        return remote(
            send_c.at[i, rows_of(peer * own, own)], recv_c.at[i, k - 1], c_send.at[i, k - 1], c_recv.at[i, k - 1], to_sub(k)
        )

    base = core * (2 * part) + col * part

    def d_copy(i, k):
        block = resid.at[i, rows_of(base + s * own, own)]
        return remote(block, block, d_send.at[i, k - 1], d_recv.at[i, k - 1], to_sub(k))

    def e2_copy(i):
        block = resid.at[i, rows_of(base, part)]
        return remote(block, block, r_send.at[2, i], r_recv.at[2, i], to_col)

    def f_copy(i):
        block = resid.at[i, rows_of(core * (2 * part), 2 * part)]
        return remote(block, block, r_send.at[3, i], r_recv.at[3, i], to_core)

    def stage_a(i):
        send_a[i] = pred[i, rows_of((1 - core) * (2 * part), 2 * part)].astype(BF16)
        a_copy(i).start()

    def stage_b(i):
        a_copy(i).wait()
        there = rows_of((1 - col) * part, part)
        here = rows_of(col * part, part)
        send_b[i] = (pred[i, rows_of(core * (2 * part) + (1 - col) * part, part)] + recv_a[i, there].astype(F32)).astype(BF16)
        b_copy(i).start()
        keep_b[i] = pred[i, rows_of(base, part)] + recv_a[i, here].astype(F32)

    def stage_c(i):
        b_copy(i).wait()
        total = keep_b[i] + recv_b[i].astype(F32)
        send_c[i] = total.astype(BF16)
        for k in hops:
            c_copy(i, k).start()
        keep_c[i] = total

    def stage_d(i):
        total = keep_c[i, rows_of(s * own, own)]
        for k in hops:
            c_copy(i, k).wait()
            total += recv_c[i, k - 1].astype(F32)
        resid[i, rows_of(base + s * own, own)] = total.astype(BF16)
        for k in hops:
            d_copy(i, k).start()

    def stage_e(i):
        for k in hops:
            d_copy(i, k).wait()
        e2_copy(i).start()

    def stage_f(i):
        e2_copy(i).wait()
        f_copy(i).start()

    def second(i):
        f_copy(i).wait()

        def add(c, carry):
            coef[c] += -step_size * jnp.dot(resid[i], full[c, i], preferred_element_type=F32)
            return carry

        lax.fori_loop(0, chunks, add, 0)

    offset = ((stage_a, 0.0), (stage_b, 1.0), (stage_c, 4.0), (stage_d, 7.5), (stage_e, 11.0), (stage_f, 14.0))
    pace = (0.2, 0.3, 1.7, 2.4, 2.6, 2.6)
    plan = [(at + pace[m] * i, m, i) for m, (stage, at) in enumerate(offset) for i in range(n_sub)]
    for _, m, i in sorted(plan):
        if m == len(offset) - 1 and i > 1:
            second(i - 2)
        offset[m][0](i)
    for i in range(max(n_sub - 2, 0), n_sub - 1):
        second(i)
    last = n_sub - 1
    f_copy(last).wait()

    def finish(c, carry):
        grad = jnp.dot(resid[last], full[c, last], preferred_element_type=F32)
        out[:, pl.ds(pl.multiple_of(c * CHUNK, CHUNK), CHUNK)] = prox(coef[c] - step_size * grad)
        return carry

    lax.fori_loop(0, chunks, finish, 0)


def transposed(n_sub, design, margins, test_ids, l1_penalty, l2_penalty):
    rows = design.shape[0]
    width = design.shape[1] // n_sub
    chunks = width // CHUNK
    tests = test_ids.shape[0]
    part = tests // 4
    own = part // n_sub
    vmem = pl.BlockSpec(memory_space=pltpu.VMEM)
    dma = pltpu.SemaphoreType.DMA
    coef_two = pl.pallas_call(
        functools.partial(kernel, n_sub, chunks),
        out_shape=jax.ShapeDtypeStruct((tests, width), F32),
        in_specs=[pl.BlockSpec(memory_space=pl.ANY)] * 2 + [vmem] * 3,
        out_specs=vmem,
        scratch_shapes=[
            pltpu.VMEM((chunks, n_sub, rows, CHUNK), BF16),
            pltpu.VMEM((n_sub, tests, rows), BF16),
            pltpu.VMEM((tests, rows), F32),
            pltpu.VMEM((n_sub, tests, rows), F32),
            pltpu.VMEM((chunks, tests, CHUNK), F32),
            pltpu.VMEM(margins.shape, F32),
            dma,
            pltpu.VMEM((n_sub, 2 * part, rows), BF16),
            pltpu.VMEM((n_sub, 2 * part, rows), BF16),
            pltpu.VMEM((n_sub, part, rows), F32),
            pltpu.VMEM((n_sub, part, rows), BF16),
            pltpu.VMEM((n_sub, part, rows), BF16),
            pltpu.VMEM((n_sub, part, rows), F32),
            pltpu.VMEM((n_sub, part, rows), BF16),
            pltpu.VMEM((n_sub, n_sub - 1, own, rows), BF16),
            pltpu.VMEM((n_sub, tests, rows), BF16),
            dma((chunks,)),
            dma((chunks, PIECES, n_sub - 1)),
            dma((chunks, PIECES, n_sub - 1)),
            dma((chunks, PIECES, n_sub - 1)),
            dma((chunks, PIECES, n_sub - 1)),
            dma((n_sub - 1,)),
            dma((n_sub - 1,)),
            dma((3, n_sub - 1)),
            dma((3, n_sub - 1)),
            dma((4, n_sub)),
            dma((4, n_sub)),
            dma((n_sub, n_sub - 1)),
            dma((n_sub, n_sub - 1)),
            dma((n_sub, n_sub - 1)),
            dma((n_sub, n_sub - 1)),
        ],
        compiler_params=pltpu.CompilerParams(
            collective_id=0, has_side_effects=True, vmem_limit_bytes=48 * 1024 * 1024
        ),
    )(design, margins, test_ids[None], l1_penalty[None], l2_penalty[None])
    return coef_two.T[None]


def solution(mesh):
    n_sub = mesh.shape["sub"]

    def local(design, margins, test_ids, l1_penalty, l2_penalty):
        width = design.shape[1] // n_sub
        fits = (
            mesh.shape["grp"] == 2
            and mesh.shape["ex"] == 4
            and n_sub > 1
            and width % CHUNK == 0
            and design.shape[0] % (32 * PIECES) == 0
            and design.shape[0] % 128 == 0
            and test_ids.shape[0] % (64 * n_sub) == 0
        )
        if fits:
            return transposed(n_sub, design, margins, test_ids, l1_penalty, l2_penalty)
        return gathered(design, margins, test_ids, l1_penalty, l2_penalty)

    in_specs = (P("sub", "ex"), P("sub", None), P("grp"), P("grp"), P("grp"))
    out_specs = P("ex", "sub", "grp")
    return jax.shard_map(local, mesh=mesh, in_specs=in_specs, out_specs=out_specs, check_vma=False)
```

```python
import functools

import jax
import jax.numpy as jnp
from jax import lax
from jax.experimental import pallas as pl
from jax.experimental.pallas import tpu as pltpu
from jax.sharding import PartitionSpec as P

step_size = 0.3
MESH = pl.DeviceIdType.MESH
CHUNK = 256
AHEAD = 2
PIECES = 2
F32 = jnp.float32
BF16 = jnp.bfloat16


def shrink(values, l1_penalty, l2_penalty):
    limit = step_size * l1_penalty
    kept = jnp.maximum(values - limit, 0.0) - jnp.maximum(-values - limit, 0.0)
    return kept / (1.0 + step_size * l2_penalty)


def gathered(design, margins, test_ids, l1_penalty, l2_penalty):
    target = jnp.take(margins, test_ids, axis=1)
    start = (-target).astype(BF16)

    def gradient_rows(resid_half):
        return lax.psum_scatter(
            lax.dot_general(design, resid_half, (((0,), (0,)), ((), ())), preferred_element_type=F32),
            "sub",
            scatter_dimension=0,
            tiled=True,
        )

    coef_one = shrink(-step_size * gradient_rows(start), l1_penalty, l2_penalty)
    predicted = jnp.dot(
        design,
        lax.all_gather(coef_one.astype(BF16), "sub", axis=0, tiled=True),
        preferred_element_type=F32,
    )
    summed = lax.psum(predicted, "ex")
    resid_half = (summed - target).astype(BF16)
    coef_two = shrink(coef_one - step_size * gradient_rows(resid_half), l1_penalty, l2_penalty)
    return coef_two[None]


def kernel(
    n_sub, chunks, design, margins, ids, l1, l2, out,
    full, start, target, pred, coef, table, table_sem,
    send_a, recv_a, keep_b, send_b, recv_b, keep_c, send_c, recv_c, resid,
    own_sem, z_send, z_recv, y_send, y_recv, s_send, s_recv, e_send, e_recv, r_send, r_recv, c_send, c_recv, d_send, d_recv,
):
    g = lax.axis_index("grp")
    s = lax.axis_index("sub")
    e = lax.axis_index("ex")
    core = lax.rem(e, 2)
    col = lax.div(e, 2)
    rows = design.shape[0]
    half = rows // 2
    tests = out.shape[0]
    width = chunks * CHUNK
    part = tests // 4
    own = part // n_sub

    def to_sub(k):
        return {"sub": lax.rem(s + k, n_sub)}

    def to_ex(j):
        return {"ex": lax.rem(e + j, 4)}

    to_core = {"ex": col * 2 + 1 - core}
    to_col = {"ex": (1 - col) * 2 + core}
    to_grp = {"grp": 1 - g}

    def remote(src, dst, send, recv, device):
        return pltpu.make_async_remote_copy(
            src_ref=src, dst_ref=dst, send_sem=send, recv_sem=recv, device_id=device, device_id_type=MESH
        )

    barrier = pltpu.get_barrier_semaphore()
    for device in [to_sub(k) for k in range(1, n_sub)] + [to_ex(j) for j in range(1, 4)] + [to_grp]:
        pl.semaphore_signal(barrier, inc=1, device_id=device, device_id_type=MESH)

    fetch = pltpu.make_async_copy(margins, table, table_sem)
    fetch.start()
    eye = lax.broadcasted_iota(jnp.int32, (tests, tests), 0) == lax.broadcasted_iota(jnp.int32, (tests, tests), 1)

    def column(row):
        return jnp.sum(jnp.where(eye, row, 0.0), axis=1, keepdims=True)

    limit = step_size * column(l1[...])
    scale = 1.0 / (1.0 + step_size * column(l2[...]))
    wanted = column(ids[...].astype(F32))
    hot = (lax.broadcasted_iota(jnp.int32, (tests, margins.shape[1]), 1).astype(F32) == wanted).astype(F32)
    fetch.wait()
    own_target = lax.dot_general(
        hot, table[...], (((1,), (1,)), ((), ())), precision=lax.Precision.HIGHEST, preferred_element_type=F32
    )
    target[...] = own_target
    start[s] = (-own_target).astype(BF16)
    first = jnp.where(e == 0, 1.0, 0.0).astype(F32)
    for i in range(n_sub):
        pred[i] = jnp.zeros(pred.shape[1:], F32)
    pred[s] = target[...] * (-first)
    pl.semaphore_wait(barrier, n_sub + 3)

    def own_copy(c):
        return pltpu.make_async_copy(
            design.at[:, pl.ds(pl.multiple_of(s * width + c * CHUNK, CHUNK), CHUNK)],
            full.at[c, s],
            own_sem.at[c],
        )

    piece = half // PIECES

    def rows_at(h):
        return pl.ds(pl.multiple_of(g * half + h * piece, 16), piece)

    def z_copy(c, h, k):
        peer = lax.rem(s + k, n_sub)
        return remote(
            design.at[rows_at(h), pl.ds(pl.multiple_of(peer * width + c * CHUNK, CHUNK), CHUNK)],
            full.at[c, s, rows_at(h)],
            z_send.at[c, h, k - 1],
            z_recv.at[c, h, k - 1],
            {"sub": peer},
        )

    def y_copy(c, h, k):
        block = full.at[c, lax.rem(s + n_sub - k, n_sub), rows_at(h)]
        return remote(block, block, y_send.at[c, h, k - 1], y_recv.at[c, h, k - 1], to_grp)

    def send_chunk(c):
        for h in range(PIECES):
            for k in hops:
                z_copy(c, h, k).start()

    hops = range(1, n_sub)
    quarter = pl.ds(pl.multiple_of(e * part, 16), part)

    def s_copy(k):
        block = start.at[s, quarter]
        return remote(block, block, s_send.at[k - 1], s_recv.at[k - 1], to_sub(k))

    def e_copy(j, k):
        block = start.at[lax.rem(s + k, n_sub), quarter]
        return remote(block, block, e_send.at[j - 1, k - 1], e_recv.at[j - 1, k - 1], to_ex(j))

    for k in hops:
        s_copy(k).start()
    for c in range(min(AHEAD, chunks)):
        send_chunk(c)
    for c in range(chunks):
        own_copy(c).start()
    for k in hops:
        s_copy(k).wait()
    for j in range(1, 4):
        for k in hops:
            e_copy(j, k).start()

    def prox(values):
        return (jnp.maximum(values - limit, 0.0) - jnp.maximum(-values - limit, 0.0)) * scale

    def pass_on(c):
        for h in range(PIECES):
            for k in hops:
                z_copy(c, h, k).wait()
                y_copy(c, h, k).start()

    def work(c, done=None):
        own_copy(c).wait()
        for h in range(PIECES):
            for k in hops:
                y_copy(c, h, k).wait()
        grad = jnp.dot(start[0], full[c, 0], preferred_element_type=F32)
        for i in range(1, n_sub):
            grad += jnp.dot(start[i], full[c, i], preferred_element_type=F32)
        one = prox(-step_size * grad)
        coef[c] = one
        one_half = one.astype(BF16)
        for i in range(n_sub):
            pred[i] += lax.dot_general(one_half, full[c, i], (((1,), (1,)), ((), ())), preferred_element_type=F32)
            if done is not None:
                done(i)

    pass_on(0)
    for j in range(1, 4):
        for k in hops:
            e_copy(j, k).wait()

    def step(c, carry):
        @pl.when(c + AHEAD - 1 < chunks)
        def _():
            send_chunk(c + AHEAD - 1)

        pass_on(c)
        work(c - 1)
        return carry

    lax.fori_loop(1, chunks, step, 0)

    def rows_of(first_row, count):
        return pl.ds(pl.multiple_of(first_row, 16), count)

    def a_copy(i):
        return remote(send_a.at[i], recv_a.at[i], r_send.at[0, i], r_recv.at[0, i], to_core)

    def b_copy(i):
        return remote(send_b.at[i], recv_b.at[i], r_send.at[1, i], r_recv.at[1, i], to_col)

    def c_copy(i, k):
        peer = lax.rem(s + k, n_sub)
        return remote(
            send_c.at[i, rows_of(peer * own, own)], recv_c.at[i, k - 1], c_send.at[i, k - 1], c_recv.at[i, k - 1], to_sub(k)
        )

    base = core * (2 * part) + col * part

    def d_copy(i, k):
        block = resid.at[i, rows_of(base + s * own, own)]
        return remote(block, block, d_send.at[i, k - 1], d_recv.at[i, k - 1], to_sub(k))

    def e2_copy(i):
        block = resid.at[i, rows_of(base, part)]
        return remote(block, block, r_send.at[2, i], r_recv.at[2, i], to_col)

    def f_copy(i):
        block = resid.at[i, rows_of(core * (2 * part), 2 * part)]
        return remote(block, block, r_send.at[3, i], r_recv.at[3, i], to_core)

    def stage_a(i):
        send_a[i] = pred[i, rows_of((1 - core) * (2 * part), 2 * part)].astype(BF16)
        a_copy(i).start()

    work(chunks - 1, stage_a)

    def stage_b(i):
        a_copy(i).wait()
        there = rows_of((1 - col) * part, part)
        here = rows_of(col * part, part)
        send_b[i] = (pred[i, rows_of(core * (2 * part) + (1 - col) * part, part)] + recv_a[i, there].astype(F32)).astype(BF16)
        b_copy(i).start()
        keep_b[i] = pred[i, rows_of(base, part)] + recv_a[i, here].astype(F32)

    def stage_c(i):
        b_copy(i).wait()
        total = keep_b[i] + recv_b[i].astype(F32)
        send_c[i] = total.astype(BF16)
        for k in hops:
            c_copy(i, k).start()
        keep_c[i] = total

    def stage_d(i):
        total = keep_c[i, rows_of(s * own, own)]
        for k in hops:
            c_copy(i, k).wait()
            total += recv_c[i, k - 1].astype(F32)
        resid[i, rows_of(base + s * own, own)] = total.astype(BF16)
        for k in hops:
            d_copy(i, k).start()

    def stage_e(i):
        for k in hops:
            d_copy(i, k).wait()
        e2_copy(i).start()

    def stage_f(i):
        e2_copy(i).wait()
        f_copy(i).start()

    def second(i):
        f_copy(i).wait()

        def add(c, carry):
            coef[c] += -step_size * jnp.dot(resid[i], full[c, i], preferred_element_type=F32)
            return carry

        lax.fori_loop(0, chunks, add, 0)

    offset = ((stage_a, 0.0), (stage_b, 1.0), (stage_c, 4.0), (stage_d, 7.5), (stage_e, 11.0), (stage_f, 14.0))
    pace = (0.2, 0.3, 1.7, 2.4, 2.6, 2.6)
    plan = [(at + pace[m] * i, m, i) for m, (stage, at) in enumerate(offset) for i in range(n_sub)]
    for _, m, i in sorted(plan):
        if m == len(offset) - 1 and i > 1:
            second(i - 2)
        if m > 0:
            offset[m][0](i)
    for i in range(max(n_sub - 2, 0), n_sub - 1):
        second(i)
    last = n_sub - 1
    f_copy(last).wait()

    def finish(c, carry):
        grad = jnp.dot(resid[last], full[c, last], preferred_element_type=F32)
        out[:, pl.ds(pl.multiple_of(c * CHUNK, CHUNK), CHUNK)] = prox(coef[c] - step_size * grad)
        return carry

    lax.fori_loop(0, chunks, finish, 0)


def transposed(n_sub, design, margins, test_ids, l1_penalty, l2_penalty):
    rows = design.shape[0]
    width = design.shape[1] // n_sub
    chunks = width // CHUNK
    tests = test_ids.shape[0]
    part = tests // 4
    own = part // n_sub
    vmem = pl.BlockSpec(memory_space=pltpu.VMEM)
    dma = pltpu.SemaphoreType.DMA
    coef_two = pl.pallas_call(
        functools.partial(kernel, n_sub, chunks),
        out_shape=jax.ShapeDtypeStruct((tests, width), F32),
        in_specs=[pl.BlockSpec(memory_space=pl.ANY)] * 2 + [vmem] * 3,
        out_specs=vmem,
        scratch_shapes=[
            pltpu.VMEM((chunks, n_sub, rows, CHUNK), BF16),
            pltpu.VMEM((n_sub, tests, rows), BF16),
            pltpu.VMEM((tests, rows), F32),
            pltpu.VMEM((n_sub, tests, rows), F32),
            pltpu.VMEM((chunks, tests, CHUNK), F32),
            pltpu.VMEM(margins.shape, F32),
            dma,
            pltpu.VMEM((n_sub, 2 * part, rows), BF16),
            pltpu.VMEM((n_sub, 2 * part, rows), BF16),
            pltpu.VMEM((n_sub, part, rows), F32),
            pltpu.VMEM((n_sub, part, rows), BF16),
            pltpu.VMEM((n_sub, part, rows), BF16),
            pltpu.VMEM((n_sub, part, rows), F32),
            pltpu.VMEM((n_sub, part, rows), BF16),
            pltpu.VMEM((n_sub, n_sub - 1, own, rows), BF16),
            pltpu.VMEM((n_sub, tests, rows), BF16),
            dma((chunks,)),
            dma((chunks, PIECES, n_sub - 1)),
            dma((chunks, PIECES, n_sub - 1)),
            dma((chunks, PIECES, n_sub - 1)),
            dma((chunks, PIECES, n_sub - 1)),
            dma((n_sub - 1,)),
            dma((n_sub - 1,)),
            dma((3, n_sub - 1)),
            dma((3, n_sub - 1)),
            dma((4, n_sub)),
            dma((4, n_sub)),
            dma((n_sub, n_sub - 1)),
            dma((n_sub, n_sub - 1)),
            dma((n_sub, n_sub - 1)),
            dma((n_sub, n_sub - 1)),
        ],
        compiler_params=pltpu.CompilerParams(
            collective_id=0, has_side_effects=True, vmem_limit_bytes=48 * 1024 * 1024
        ),
    )(design, margins, test_ids[None], l1_penalty[None], l2_penalty[None])
    return coef_two.T[None]


def solution(mesh):
    n_sub = mesh.shape["sub"]

    def local(design, margins, test_ids, l1_penalty, l2_penalty):
        width = design.shape[1] // n_sub
        fits = (
            mesh.shape["grp"] == 2
            and mesh.shape["ex"] == 4
            and n_sub > 1
            and width % CHUNK == 0
            and design.shape[0] % (32 * PIECES) == 0
            and design.shape[0] % 128 == 0
            and test_ids.shape[0] % (64 * n_sub) == 0
        )
        if fits:
            return transposed(n_sub, design, margins, test_ids, l1_penalty, l2_penalty)
        return gathered(design, margins, test_ids, l1_penalty, l2_penalty)

    in_specs = (P("sub", "ex"), P("sub", None), P("grp"), P("grp"), P("grp"))
    out_specs = P("ex", "sub", "grp")
    return jax.shard_map(local, mesh=mesh, in_specs=in_specs, out_specs=out_specs, check_vma=False)
```
